256 devices in a mesh: branch: 8 (over y, z_hi), fsdp: 32 (over x, z_lo, core).
Axes of the slice: x: 4, y: 4, z: 8 (z_hi: 2, z_lo: 4; z = z_hi * 4 + z_lo), core: 2. Of those that a mesh axis runs over, the one named last changes fastest.
Arguments:
- inputs: bfloat16 [8, 4, 128, 4096], P('branch', None, 'fsdp'), may hold values from -6 to 6
- targets: bfloat16 [8, 4, 128, 4096], P('branch', None, 'fsdp'), may hold values from -6 to 6
- gain: float32 [8, 4096], P('branch'), may hold values from 0.5 to 2
- w_gate: bfloat16 [8, 4096, 8192], P('branch', None, 'fsdp'), may hold values from -4 to 4
- w_up: bfloat16 [8, 4096, 8192], P('branch', None, 'fsdp'), may hold values from -4 to 4
- w_down: bfloat16 [8, 8192, 4096], P('branch', 'fsdp'), may hold values from -4 to 4
Outputs:
- merged_gate: float32 [4096, 8192], P('branch', 'fsdp')
- merged_up: float32 [4096, 8192], P('branch', 'fsdp')
- merged_down: float32 [8192, 4096], P('fsdp', 'branch')
The draws below stay inside these ranges and needn't reach their ends.
All inputs are finite; a program needn't handle non-finite values.
Results may differ from the reference program's by a relative error of at most 0.025.
Values may be sent and summed in bfloat16 or wider, within the bound.
No kernel may reach another device: no remote copies, remote signals or barrier semaphores. Data moves between devices by JAX's collectives and lax.ppermute only.
A program may use at most 128 MiB of HBM per device.

```python
import math
import jax
import jax.numpy as jnp
from jax import lax

D = 4096
FWIN = 8192
MB = 4
MTOK = 128
BRANCHES = 8


def level_of(key, extent, split, low, top_value):
    loudness = 1.0
    for axis_at, parts in split:
        heights = jax.random.uniform(jax.random.fold_in(jax.random.fold_in(key, 6), axis_at), (parts,), jnp.float32, low / len(split), top_value / len(split))
        loudness = loudness * jnp.repeat(jnp.exp(heights), extent[axis_at] // parts).reshape((-1,) + (1,) * (len(extent) - 1 - axis_at))
    return loudness


def centred(key, extent, deviation, limit, cuts=(), dtype=jnp.bfloat16):
    drawn = deviation * jax.random.normal(key, extent, jnp.float32)
    if cuts:
        drawn = drawn * level_of(key, extent, cuts, -0.22, 0.18)
    return jnp.clip(drawn, -limit, limit).astype(dtype)


def setup_inputs(seed: int = 0) -> dict:
    key_of = jax.random.split(jax.random.key(seed), 7)
    return {
        "inputs": centred(key_of[0], (BRANCHES, MB, MTOK, D), 1.0, 6.0, ((0, 8), (2, 32))),
        "targets": centred(key_of[1], (BRANCHES, MB, MTOK, D), 1.0, 6.0, ((0, 8), (2, 32))),
        "gain": jnp.clip(jnp.exp(math.log(2.0) - 1.3862944 * jax.random.uniform(key_of[2], (BRANCHES, D), jnp.float32) ** level_of(key_of[2], (BRANCHES, D), ((0, 8),), -0.2, 0.2)), 0.5, 2.0),
        "w_gate": centred(key_of[3], (BRANCHES, D, FWIN), 1.0, 4.0, ((0, 8), (2, 32))),
        "w_up": centred(key_of[4], (BRANCHES, D, FWIN), 1.0, 4.0, ((0, 8), (2, 32))),
        "w_down": centred(key_of[5], (BRANCHES, FWIN, D), 1.0, 4.0, ((0, 8), (1, 32))),
    }


def branch_terms(batch_in, batch_target, gain_row, gate_mat, up_mat, down_mat):
    scale_model = 1.0 / math.sqrt(D)
    scale_hidden = 1.0 / math.sqrt(FWIN)
    sq_gate = jnp.zeros(gate_mat.shape, jnp.float32)
    sq_up = jnp.zeros(up_mat.shape, jnp.float32)
    sq_down = jnp.zeros(down_mat.shape, jnp.float32)
    for item in range(MB):
        x_rows = batch_in[item]
        gate_pre = jnp.dot(x_rows, gate_mat, preferred_element_type=jnp.float32) * scale_model
        up_pre = jnp.dot(x_rows, up_mat, preferred_element_type=jnp.float32) * scale_model
        sig_gate = jax.nn.sigmoid(gate_pre)
        act_gate = gate_pre * sig_gate
        hidden = (act_gate * up_pre).astype(jnp.bfloat16)
        out_rows = x_rows.astype(jnp.float32) + jnp.dot(hidden, down_mat, preferred_element_type=jnp.float32) * scale_hidden
        recip = lax.rsqrt(lax.optimization_barrier(jnp.mean(out_rows * out_rows, axis=-1, keepdims=True)) + 1e-05)
        normed = out_rows * recip * gain_row
        delta = normed - batch_target[item].astype(jnp.float32)
        center = lax.optimization_barrier(jnp.mean(delta * gain_row * out_rows, axis=-1, keepdims=True))
        grad_out = (gain_row * recip * delta - recip * recip * recip * out_rows * center).astype(jnp.bfloat16)
        grad_hidden = lax.dot_general(grad_out, down_mat, (((1,), (1,)), ((), ())), preferred_element_type=jnp.float32) * scale_hidden
        grad_down = lax.dot_general(hidden, grad_out, (((0,), (0,)), ((), ())), preferred_element_type=jnp.float32) * scale_hidden
        d_gate = (grad_hidden * up_pre * sig_gate * (1.0 + gate_pre * (1.0 - sig_gate))).astype(jnp.bfloat16)
        d_up = (grad_hidden * act_gate).astype(jnp.bfloat16)
        grad_gate = lax.dot_general(x_rows, d_gate, (((0,), (0,)), ((), ())), preferred_element_type=jnp.float32) * scale_model
        grad_up = lax.dot_general(x_rows, d_up, (((0,), (0,)), ((), ())), preferred_element_type=jnp.float32) * scale_model
        sq_gate = sq_gate + grad_gate * grad_gate
        sq_up = sq_up + grad_up * grad_up
        sq_down = sq_down + grad_down * grad_down
    result = []
    for fisher, mat in ((sq_gate / MB, gate_mat), (sq_up / MB, up_mat), (sq_down / MB, down_mat)):
        result.append((fisher * mat.astype(jnp.float32)).astype(jnp.bfloat16).astype(jnp.float32))
        result.append(fisher.astype(jnp.bfloat16).astype(jnp.float32))
    return tuple(result)

def reference(inputs, targets, gain, w_gate, w_up, w_down):

    def step(carry, pieces):
        terms = branch_terms(*pieces)
        return (tuple((a + b for a, b in zip(carry, terms))), None)
    start = (jnp.zeros((D, FWIN), jnp.float32), jnp.zeros((D, FWIN), jnp.float32), jnp.zeros((D, FWIN), jnp.float32), jnp.zeros((D, FWIN), jnp.float32), jnp.zeros((FWIN, D), jnp.float32), jnp.zeros((FWIN, D), jnp.float32))
    totals, _ = lax.scan(step, start, (inputs, targets, gain, w_gate, w_up, w_down))
    return (totals[0] / totals[1], totals[2] / totals[3], totals[4] / totals[5])
```

```python
import functools
import math

import jax
import jax.numpy as jnp
from jax import lax
from jax.experimental import pallas as pl
from jax.experimental.pallas import tpu as pltpu
from jax.sharding import PartitionSpec as P

F32 = jnp.float32
BF16 = jnp.bfloat16

SIZES = {"branch": (("y", 4), ("zh", 2)), "fsdp": (("x", 4), ("zl", 4), ("core", 2))}


def _ring(axis, name, shift):
    parts = SIZES[axis]
    total = math.prod(size for _, size in parts)
    stride = 1
    for part, size in reversed(parts):
        if part == name:
            break
        stride *= size
    pairs = []
    for i in range(total):
        at = (i // stride) % size
        pairs.append((i, i + ((at + shift) % size - at) * stride))
    return pairs


def shift(value, name, by):
    axis = "branch" if name in ("y", "zh") else "fsdp"
    return lax.ppermute(value, axis, _ring(axis, name, by))


RELATIVE = (1, 3, 2)


def gather(value, name):
    return jnp.concatenate([value] + [shift(value, name, by) for by in RELATIVE], axis=0)


def scatter(value, name):
    rows = value.shape[0] // 4
    total = value[:rows].astype(F32)
    back = [
        shift(value[(i + 1) * rows : (i + 2) * rows], name, -by) for i, by in enumerate(RELATIVE)
    ]
    for piece in back:
        total = total + piece.astype(F32)
    return total.astype(BF16)


def gather_rows(block):
    own = gather(gather(block, "zl"), "x")
    return own, shift(own, "core", 1)


def scatter_rows(own, other):
    chip = (own.astype(F32) + shift(other, "core", 1).astype(F32)).astype(BF16)
    return scatter(scatter(chip, "x"), "zl")


def pair_up(rows, core):
    mine = lax.dynamic_slice_in_dim(rows, 2 * core, 2, 0)
    theirs = lax.dynamic_slice_in_dim(rows, 2 - 2 * core, 2, 0)
    return jnp.concatenate([mine, shift(theirs, "core", 1)], axis=1)


def norm_grad(out_rows, target_rows, gain_row):
    recip = lax.rsqrt(jnp.mean(out_rows * out_rows, axis=-1, keepdims=True) + 1e-05)
    normed = out_rows * recip * gain_row
    delta = normed - target_rows
    center = jnp.mean(delta * gain_row * out_rows, axis=-1, keepdims=True)
    return (gain_row * recip * delta - recip * recip * recip * out_rows * center).astype(BF16)


def _fisher_kernel(slot_ref, *refs, factor):
    del slot_ref
    out_ref = refs[-1]
    half = (len(refs) - 1) // 2
    total = None
    for left_ref, right_ref in zip(refs[:half], refs[half:-1]):
        grad = lax.dot_general(
            left_ref[...], right_ref[...], (((0,), (0,)), ((), ())), preferred_element_type=F32
        )
        total = grad * grad if total is None else total + grad * grad
    out_ref[...] = (total * factor).astype(BF16)


def fisher_block(slot, lefts, rights, factor, wide):
    tile = 256
    count = 1024 // tile
    tokens = lefts[0].shape[0]

    def cut(i, slot_ref):
        return (0, slot_ref[0] * count + i)

    def whole(i, slot_ref):
        return (0, 0)

    cut_spec = pl.BlockSpec((tokens, tile), cut)
    if wide == 0:
        specs = [cut_spec] * len(lefts)
        specs += [pl.BlockSpec(r.shape, whole) for r in rights]
        out_shape = (1024, rights[0].shape[1])
        out_spec = pl.BlockSpec((tile, rights[0].shape[1]), lambda i, slot_ref: (i, 0))
    else:
        specs = [pl.BlockSpec(r.shape, whole) for r in lefts]
        specs += [cut_spec] * len(rights)
        out_shape = (lefts[0].shape[1], 1024)
        out_spec = pl.BlockSpec((lefts[0].shape[1], tile), lambda i, slot_ref: (0, i))
    macs = len(lefts) * tokens * out_shape[0] * out_shape[1]
    return pl.pallas_call(
        functools.partial(_fisher_kernel, factor=factor),
        grid_spec=pltpu.PrefetchScalarGridSpec(
            num_scalar_prefetch=1, grid=(count,), in_specs=specs, out_specs=out_spec
        ),
        out_shape=jax.ShapeDtypeStruct(out_shape, BF16),
        cost_estimate=pl.CostEstimate(
            flops=2 * macs, bytes_accessed=4 * 1024 * 1024, transcendentals=0
        ),
    )(slot, *lefts, *rights)


def body(inputs, targets, gain, w_gate, w_up, w_down):
    gain_row = gain[0]
    gate_mat, up_mat, down_mat = w_gate[0], w_up[0], w_down[0]
    scale_model = 1.0 / math.sqrt(inputs.shape[3])
    scale_hidden = 1.0 / math.sqrt(w_down.shape[1] * 32)
    core = lax.axis_index("fsdp") % 2
    branch = lax.axis_index("branch")
    y_at, zh_at = branch // 2, branch % 2

    def slot_of(by):
        return (y_at + by) % 4

    x_pair = pair_up(inputs[0], core)
    target_pair = pair_up(targets[0], core)

    def fetch(mat, axis):
        own = lax.dynamic_slice_in_dim(mat, slot_of(0) * 1024, 1024, axis)
        rest = [
            shift(lax.dynamic_slice_in_dim(mat, slot_of(by) * 1024, 1024, axis), "y", by)
            for by in RELATIVE
        ]
        return [own] + rest

    lines = [fetch(down_mat, 1), fetch(gate_mat, 0), fetch(up_mat, 0)]

    tokens, hiddens, grads, pres = [], [], [], []
    for j in range(2):
        own, other = gather_rows(x_pair[j])
        partial = []
        tokens += [own, other]
        for rows in (own, other):
            gate_pre = jnp.dot(rows, gate_mat, preferred_element_type=F32) * scale_model
            up_pre = jnp.dot(rows, up_mat, preferred_element_type=F32) * scale_model
            hidden = (gate_pre * jax.nn.sigmoid(gate_pre) * up_pre).astype(BF16)
            partial.append(
                (jnp.dot(hidden, down_mat, preferred_element_type=F32) * scale_hidden).astype(BF16)
            )
            hiddens.append(hidden)
            pres.append((gate_pre, up_pre))
        summed = scatter_rows(*partial)
        out_rows = x_pair[j].astype(F32) + summed.astype(F32)
        grads += gather_rows(norm_grad(out_rows, target_pair[j].astype(F32), gain_row))

    d_gates, d_ups = [], []
    for grad_out, (gate_pre, up_pre) in zip(grads, pres):
        grad_hidden = (
            lax.dot_general(
                grad_out, down_mat, (((1,), (1,)), ((), ())), preferred_element_type=F32
            )
            * scale_hidden
        )
        sig = jax.nn.sigmoid(gate_pre)
        d_gates.append(
            (grad_hidden * up_pre * sig * (1.0 + gate_pre * (1.0 - sig))).astype(BF16)
        )
        d_ups.append((grad_hidden * gate_pre * sig).astype(BF16))

    def merge(lefts, rights, scale, wide, line):
        def block(by):
            slot = jnp.reshape(slot_of(by), (1,)).astype(jnp.int32)
            return fisher_block(slot, lefts, rights, scale * scale / 4, wide)

        fishers = [None] + [shift(block(by), "y", by) for by in RELATIVE]
        fishers[0] = block(0)

        def sums(half):
            num, den = 0.0, 0.0
            for fisher, mat in zip(fishers, line):
                part = lax.dynamic_slice_in_dim(fisher, half * 512, 512, wide).astype(F32)
                num = num + part * lax.dynamic_slice_in_dim(mat, half * 512, 512, wide).astype(F32)
                den = den + part
            return num, den

        away = jnp.stack(sums(1 - zh_at)).astype(BF16)
        back = shift(away, "zh", 1).astype(F32)
        num, den = sums(zh_at)
        return (num + back[0]) / (den + back[1])

    down = merge(hiddens, grads, scale_hidden, 1, lines[0])
    gate = merge(tokens, d_gates, scale_model, 0, lines[1])
    up = merge(tokens, d_ups, scale_model, 0, lines[2])
    return gate, up, down


def solution(mesh):
    placed = (
        P("branch", None, "fsdp", None),
        P("branch", None, "fsdp", None),
        P("branch", None),
        P("branch", None, "fsdp"),
        P("branch", None, "fsdp"),
        P("branch", "fsdp", None),
    )
    return jax.shard_map(
        body,
        mesh=mesh,
        in_specs=placed,
        out_specs=(P("branch", "fsdp"), P("branch", "fsdp"), P("fsdp", "branch")),
        check_vma=False,
    )
```

```python
import functools
import math

import jax
import jax.numpy as jnp
from jax import lax
from jax.experimental import pallas as pl
from jax.experimental.pallas import tpu as pltpu
from jax.sharding import PartitionSpec as P

F32 = jnp.float32
BF16 = jnp.bfloat16

SIZES = {"branch": (("y", 4), ("zh", 2)), "fsdp": (("x", 4), ("zl", 4), ("core", 2))}


def _ring(axis, name, shift):
    parts = SIZES[axis]
    total = math.prod(size for _, size in parts)
    stride = 1
    for part, size in reversed(parts):
        if part == name:
            break
        stride *= size
    pairs = []
    for i in range(total):
        at = (i // stride) % size
        pairs.append((i, i + ((at + shift) % size - at) * stride))
    return pairs


def shift(value, name, by):
    axis = "branch" if name in ("y", "zh") else "fsdp"
    return lax.ppermute(value, axis, _ring(axis, name, by))


RELATIVE = (1, 3, 2)


def tie(*values):
    return lax.optimization_barrier(values)


def gather(value, name):
    return [value] + [shift(value, name, by) for by in RELATIVE]


def scatter(parts, name):
    back = [shift(part, name, -by) for by, part in zip(RELATIVE, parts[1:])]
    total = parts[0].astype(F32)
    for piece in back:
        total = total + piece.astype(F32)
    return total.astype(BF16)


def gather_line(rows):
    return jnp.concatenate(gather(rows, "zl"), axis=1)


def pair_up(rows, core):
    mine = lax.dynamic_slice_in_dim(rows, 2 * core, 2, 1)
    theirs = lax.dynamic_slice_in_dim(rows, 2 - 2 * core, 2, 1)
    return jnp.concatenate([mine, shift(theirs, "core", 1)], axis=2)


def norm_grad(out_rows, target_rows, gain_row):
    recip = lax.rsqrt(jnp.mean(out_rows * out_rows, axis=-1, keepdims=True) + 1e-05)
    normed = out_rows * recip * gain_row
    delta = normed - target_rows
    center = jnp.mean(delta * gain_row * out_rows, axis=-1, keepdims=True)
    return (gain_row * recip * delta - recip * recip * recip * out_rows * center).astype(BF16)


def _fisher_kernel(slots_ref, *refs, jobs, count, tile):
    del slots_ref
    ins, outs = refs[:-count], refs[-count:]

    def rows(ref, item, at=None):
        piece = ref[:, item] if at is None else ref[:, item, :, at : at + tile]
        return piece.reshape(piece.shape[0] * piece.shape[1], piece.shape[2])

    for at_out, out_ref in enumerate(outs):

        @pl.when(pl.program_id(0) == at_out)
        def _(out_ref=out_ref):
            base = 0
            for job, factor in enumerate(jobs):
                lefts, rights = ins[4 * job : 4 * job + 2], ins[4 * job + 2 : 4 * job + 4]
                height = lefts[0].shape[3]
                for at in range(0, height, tile):
                    total = None
                    for left_ref, right_ref in zip(lefts, rights):
                        for item in range(left_ref.shape[1]):
                            grad = lax.dot_general(
                                rows(left_ref, item, at),
                                rows(right_ref, item),
                                (((0,), (0,)), ((), ())),
                                preferred_element_type=F32,
                            )
                            total = grad * grad if total is None else total + grad * grad
                    out_ref[base + at : base + at + tile, :] = (total * factor).astype(BF16)
                base += height


def fisher_blocks(slots, *jobs):
    count = slots.shape[0]
    specs, operands, factors = [], [], []
    height, width = 0, 0
    for lefts, rights, scale, wide in jobs:
        lead = lefts[0].shape[:3]
        cut = pl.BlockSpec(lead + (512,), lambda i, slots_ref: (0, 0, 0, slots_ref[i]))
        held = pl.BlockSpec((lefts if wide else rights)[0].shape, lambda i, slots_ref: (0, 0, 0, 0))
        specs += [held, held, cut, cut] if wide else [cut, cut, held, held]
        operands += [*lefts, *rights]
        factors.append(scale * scale / 4)
        height += lefts[0].shape[3] if wide else 512
        width = 512 if wide else rights[0].shape[3]
    out_shape = (height, width)
    return pl.pallas_call(
        functools.partial(_fisher_kernel, jobs=tuple(factors), count=count, tile=256),
        grid_spec=pltpu.PrefetchScalarGridSpec(
            num_scalar_prefetch=1,
            grid=(count,),
            in_specs=specs,
            out_specs=[pl.BlockSpec(out_shape, lambda i, slots_ref: (0, 0))] * count,
        ),
        out_shape=[jax.ShapeDtypeStruct(out_shape, BF16)] * count,
        compiler_params=pltpu.CompilerParams(vmem_limit_bytes=48 * 1024 * 1024),
        cost_estimate=pl.CostEstimate(flops=1, bytes_accessed=1, transcendentals=0),
    )(slots, *operands)


def _sums(fisher_refs, mat_refs):
    num, den = 0.0, 0.0
    for fisher_ref, mat_ref in zip(fisher_refs, mat_refs):
        part = fisher_ref[...].astype(F32)
        num = num + part * mat_ref[...].astype(F32)
        den = den + part
    return num, den


def _away_kernel(half_ref, *refs):
    del half_ref
    num, den = _sums(refs[:4], refs[4:8])
    refs[8][0] = num.astype(BF16)
    refs[8][1] = den.astype(BF16)


def _merge_kernel(half_ref, *refs):
    del half_ref
    both, down, both_mats, down_mats = (refs[4 * i : 4 * i + 4] for i in range(4))
    gate_back, up_back, down_back, gate_ref, up_ref, down_ref = refs[16:]

    def merge(num, den, back):
        return (num + back[0].astype(F32)) / (den + back[1].astype(F32))

    num, den = _sums(both, both_mats)
    gate_ref[...] = merge(num[:, :256], den[:, :256], gate_back)
    up_ref[...] = merge(num[:, 256:], den[:, 256:], up_back)
    num, den = _sums(down, down_mats)
    down_ref[...] = merge(num, den, down_back)


STEPS = 2


def _rows(height, width, base=0):
    return pl.BlockSpec((height // STEPS, width), lambda i, half_ref: (base + i, 0))


def _pair(height, width):
    return pl.BlockSpec((2, height // STEPS, width), lambda i, half_ref: (0, i, 0))


def _half_rows(height, width, column=0):
    return pl.BlockSpec(
        (height // STEPS, width), lambda i, half_ref: (half_ref[0] * STEPS + i, column)
    )


def _half_columns(height, width):
    return pl.BlockSpec((height // STEPS, width), lambda i, half_ref: (i, half_ref[0]))


def _call(kernel, half, operands, in_specs, out_shapes, out_specs):
    return pl.pallas_call(
        kernel,
        grid_spec=pltpu.PrefetchScalarGridSpec(
            num_scalar_prefetch=1, grid=(STEPS,), in_specs=in_specs, out_specs=out_specs
        ),
        out_shape=out_shapes,
        cost_estimate=pl.CostEstimate(flops=1, bytes_accessed=1, transcendentals=0),
    )(half, *operands)


def leaving(half, fishers, mats, mat_spec):
    height, width = fishers[0].shape
    return _call(
        _away_kernel,
        half,
        [*fishers, *mats],
        [_rows(height, width)] * 4 + [mat_spec] * 4,
        [jax.ShapeDtypeStruct((2, height, width), BF16)],
        [_pair(height, width)],
    )[0]


def merged(half, owns, both_line, down_line, gate_back, up_back, down_back):
    return _call(
        _merge_kernel,
        half,
        [*owns, *owns, *both_line, *down_line, gate_back, up_back, down_back],
        [_rows(512, 512)] * 4
        + [_rows(256, 512, 512 // (256 // STEPS))] * 4
        + [_half_rows(512, 512)] * 4
        + [_half_columns(256, 512)] * 4
        + [_pair(512, 256), _pair(512, 256), _pair(256, 512)],
        [
            jax.ShapeDtypeStruct((512, 256), F32),
            jax.ShapeDtypeStruct((512, 256), F32),
            jax.ShapeDtypeStruct((256, 512), F32),
        ],
        [_rows(512, 256), _rows(512, 256), _rows(256, 512)],
    )


def body(inputs, targets, gain, w_gate, w_up, w_down):
    gain_row = gain[0]
    down_mat = w_down[0]
    width = inputs.shape[3]
    scale_model = 1.0 / math.sqrt(width)
    scale_hidden = 1.0 / math.sqrt(w_down.shape[1] * 32)
    core = lax.axis_index("fsdp") % 2
    branch = lax.axis_index("branch")
    y_at, zh_at = branch // 2, branch % 2
    zh_own = jnp.reshape(zh_at, (1,)).astype(jnp.int32)
    zh_away = 1 - zh_own

    def slot_of(by):
        return (y_at + by) % 4

    def slices(mat, axis):
        return [
            lax.dynamic_slice_in_dim(mat, slot_of(by) * 1024, 1024, axis) for by in (0,) + RELATIVE
        ]

    def fetch(part, by):
        return shift(part, "y", by)

    pairs = pair_up(jnp.stack([inputs[0], targets[0]]), core)
    x_pair, target_pair = pairs[0], pairs[1]

    line = gather_line(x_pair)
    line, down_mat_late = tie(line, down_mat)
    down_parts = slices(down_mat_late, 1)
    down_line = down_parts[:1] + [fetch(p, by) for by, p in zip(RELATIVE, down_parts[1:])]
    both_mat = jnp.concatenate([w_gate[0], w_up[0]], axis=1)
    tokens = jnp.stack(gather(line, "x"))
    tokens, down_line, both_mat = tie(tokens, down_line, both_mat)
    both_parts = slices(both_mat, 0)
    near = [fetch(both_parts[1], 1), fetch(both_parts[2], 3)]
    tokens = [tokens, shift(tokens, "core", 1)]

    def times(left, mat, scale):
        return jnp.einsum("xkmd,df->xkmf", left, mat, preferred_element_type=F32) * scale

    def forward(rows):
        pre = times(rows, both_mat, scale_model)
        gate_pre, up_pre = pre[..., :256], pre[..., 256:]
        hidden = (gate_pre * jax.nn.sigmoid(gate_pre) * up_pre).astype(BF16)
        return pre, hidden, times(hidden, down_mat, scale_hidden).astype(BF16)

    steps = [forward(rows) for rows in tokens]
    hiddens = [step[1] for step in steps]
    chip = (steps[0][2].astype(F32) + shift(steps[1][2], "core", 1).astype(F32)).astype(BF16)
    chip = scatter([chip[i] for i in range(4)], "x")
    chip, near, far = tie(chip, near, both_parts[3])
    far = fetch(far, 2)
    summed = scatter([chip[:, 8 * i : 8 * i + 8] for i in range(4)], "zl")
    out_rows = x_pair.astype(F32) + summed.astype(F32)
    grad_local = norm_grad(out_rows, target_pair.astype(F32), gain_row)
    grads = jnp.stack(gather(gather_line(grad_local), "x"))
    grads, far = tie(grads, far)
    both_line = [both_parts[0]] + near + [far]
    grads = [grads, shift(grads, "core", 1)]

    def blocks(half, *jobs):
        slots = jnp.concatenate([2 * slot_of(by) + half for by in RELATIVE + (0,)])
        return fisher_blocks(slots, *jobs)

    def exchange(parts):
        return [parts[3]] + [shift(part, "y", by) for by, part in zip(RELATIVE, parts)]

    down_away = blocks(zh_away, (hiddens, grads, scale_hidden, 1))
    grads, down_away = tie(grads, down_away)
    down_away = exchange(down_away)

    d_gates, d_ups = [], []
    for grad_out, (pre, _, _) in zip(grads, steps):
        grad_hidden = (
            jnp.einsum("xkmd,fd->xkmf", grad_out, down_mat, preferred_element_type=F32)
            * scale_hidden
        )
        gate_pre, up_pre = pre[..., :256], pre[..., 256:]
        sig = jax.nn.sigmoid(gate_pre)
        d_gates.append(
            (grad_hidden * up_pre * sig * (1.0 + gate_pre * (1.0 - sig))).astype(BF16)
        )
        d_ups.append((grad_hidden * gate_pre * sig).astype(BF16))
    gate_away = blocks(zh_away, (tokens, d_gates, scale_model, 0))

    (down_away, gate_away, hiddens, grads, tokens, d_gates, d_ups) = tie(
        down_away, gate_away, hiddens, grads, tokens, d_gates, d_ups
    )
    down_sent = leaving(zh_away, down_away, down_line, _half_columns(256, 512))
    down_sent, gate_away, tokens, d_ups = tie(down_sent, gate_away, tokens, d_ups)
    down_back = shift(down_sent, "zh", 1)
    gate_away = exchange(gate_away)
    up_away = blocks(zh_away, (tokens, d_ups, scale_model, 0))

    gate_away, up_away, hiddens, grads, tokens, d_gates, d_ups = tie(
        gate_away, up_away, hiddens, grads, tokens, d_gates, d_ups
    )
    gate_sent = leaving(zh_away, gate_away, both_line, _half_rows(512, 256))
    gate_sent, up_away, hiddens, grads, tokens, d_gates, d_ups = tie(
        gate_sent, up_away, hiddens, grads, tokens, d_gates, d_ups
    )
    gate_back = shift(gate_sent, "zh", 1)
    up_away = exchange(up_away)
    d_both = [jnp.concatenate(pair, axis=-1) for pair in zip(d_gates, d_ups)]
    own = blocks(
        zh_own, (tokens, d_both, scale_model, 0), (hiddens, grads, scale_hidden, 1)
    )

    up_away, own, down_back = tie(up_away, own, down_back)
    up_sent = leaving(zh_away, up_away, both_line, _half_rows(512, 256, 1))
    up_sent, own = tie(up_sent, own)
    far_own, gate_back = tie(own[2], gate_back)
    own = [own[0], own[1], far_own, own[3]]
    up_back = shift(up_sent, "zh", 1)
    owns = exchange(own)
    gate, up, down = merged(zh_own, owns, both_line, down_line, gate_back, up_back, down_back)
    return gate, up, down


def solution(mesh):
    placed = (
        P("branch", None, "fsdp", None),
        P("branch", None, "fsdp", None),
        P("branch", None),
        P("branch", None, "fsdp"),
        P("branch", None, "fsdp"),
        P("branch", "fsdp", None),
    )
    return jax.shard_map(
        body,
        mesh=mesh,
        in_specs=placed,
        out_specs=(P("branch", "fsdp"), P("branch", "fsdp"), P("fsdp", "branch")),
        check_vma=False,
    )
```

```python
import functools
import math

import jax
import jax.numpy as jnp
from jax import lax
from jax.experimental import pallas as pl
from jax.experimental.pallas import tpu as pltpu
from jax.sharding import PartitionSpec as P

F32 = jnp.float32
BF16 = jnp.bfloat16

SIZES = {"branch": (("y", 4), ("zh", 2)), "fsdp": (("x", 4), ("zl", 4), ("core", 2))}


def _ring(axis, name, shift):
    parts = SIZES[axis]
    total = math.prod(size for _, size in parts)
    stride = 1
    for part, size in reversed(parts):
        if part == name:
            break
        stride *= size
    pairs = []
    for i in range(total):
        at = (i // stride) % size
        pairs.append((i, i + ((at + shift) % size - at) * stride))
    return pairs


def shift(value, name, by):
    axis = "branch" if name in ("y", "zh") else "fsdp"
    return lax.ppermute(value, axis, _ring(axis, name, by))


RELATIVE = (1, 3, 2)


def tie(*values):
    return lax.optimization_barrier(values)


def gather(value, name):
    return [value] + [shift(value, name, by) for by in RELATIVE]


def scatter(parts, name):
    back = [shift(part, name, -by) for by, part in zip(RELATIVE, parts[1:])]
    total = parts[0].astype(F32)
    for piece in back:
        total = total + piece.astype(F32)
    return total.astype(BF16)


def gather_line(rows):
    return jnp.concatenate(gather(rows, "zl"), axis=1)


def pair_up(rows, core):
    mine = lax.dynamic_slice_in_dim(rows, 2 * core, 2, 0)
    theirs = lax.dynamic_slice_in_dim(rows, 2 - 2 * core, 2, 0)
    return lax.optimization_barrier(
        jnp.concatenate([mine, shift(theirs, "core", 1)], axis=1)
    )


def norm_grad(out_rows, target_rows, gain_row):
    recip = lax.rsqrt(jnp.mean(out_rows * out_rows, axis=-1, keepdims=True) + 1e-05)
    normed = out_rows * recip * gain_row
    delta = normed - target_rows
    center = jnp.mean(delta * gain_row * out_rows, axis=-1, keepdims=True)
    return (gain_row * recip * delta - recip * recip * recip * out_rows * center).astype(BF16)


def _fisher_kernel(slots_ref, *refs, jobs, count, tile):
    del slots_ref
    ins, outs = refs[:-count], refs[-count:]

    def rows(ref, item, at=None):
        piece = ref[:, item] if at is None else ref[:, item, :, at : at + tile]
        return piece.reshape(piece.shape[0] * piece.shape[1], piece.shape[2])

    for at_out, out_ref in enumerate(outs):

        @pl.when(pl.program_id(0) == at_out)
        def _(out_ref=out_ref):
            base = 0
            for job, factor in enumerate(jobs):
                lefts, rights = ins[4 * job : 4 * job + 2], ins[4 * job + 2 : 4 * job + 4]
                height = lefts[0].shape[3]
                for at in range(0, height, tile):
                    total = None
                    for left_ref, right_ref in zip(lefts, rights):
                        for item in range(left_ref.shape[1]):
                            grad = lax.dot_general(
                                rows(left_ref, item, at),
                                rows(right_ref, item),
                                (((0,), (0,)), ((), ())),
                                preferred_element_type=F32,
                            )
                            total = grad * grad if total is None else total + grad * grad
                    out_ref[base + at : base + at + tile, :] = (total * factor).astype(BF16)
                base += height


def fisher_blocks(slots, *jobs):
    count = slots.shape[0]
    specs, operands, factors = [], [], []
    height, width = 0, 0
    for lefts, rights, scale, wide in jobs:
        lead = lefts[0].shape[:3]
        cut = pl.BlockSpec(lead + (512,), lambda i, slots_ref: (0, 0, 0, slots_ref[i]))
        held = pl.BlockSpec((lefts if wide else rights)[0].shape, lambda i, slots_ref: (0, 0, 0, 0))
        specs += [held, held, cut, cut] if wide else [cut, cut, held, held]
        operands += [*lefts, *rights]
        factors.append(scale * scale / 4)
        height += lefts[0].shape[3] if wide else 512
        width = 512 if wide else rights[0].shape[3]
    out_shape = (height, width)
    return pl.pallas_call(
        functools.partial(_fisher_kernel, jobs=tuple(factors), count=count, tile=256),
        grid_spec=pltpu.PrefetchScalarGridSpec(
            num_scalar_prefetch=1,
            grid=(count,),
            in_specs=specs,
            out_specs=[pl.BlockSpec(out_shape, lambda i, slots_ref: (0, 0))] * count,
        ),
        out_shape=[jax.ShapeDtypeStruct(out_shape, BF16)] * count,
        compiler_params=pltpu.CompilerParams(vmem_limit_bytes=48 * 1024 * 1024),
        cost_estimate=pl.CostEstimate(flops=1, bytes_accessed=1, transcendentals=0),
    )(slots, *operands)


def _sums(fisher_refs, mat_refs):
    num, den = 0.0, 0.0
    for fisher_ref, mat_ref in zip(fisher_refs, mat_refs):
        part = fisher_ref[...].astype(F32)
        num = num + part * mat_ref[...].astype(F32)
        den = den + part
    return num, den


def _away_kernel(half_ref, *refs):
    del half_ref
    num, den = _sums(refs[:4], refs[4:8])
    refs[8][0] = num.astype(BF16)
    refs[8][1] = den.astype(BF16)


def _merge_kernel(half_ref, *refs):
    del half_ref
    both, down, both_mats, down_mats = (refs[4 * i : 4 * i + 4] for i in range(4))
    gate_back, up_back, down_back, gate_ref, up_ref, down_ref = refs[16:]

    def merge(num, den, back):
        return (num + back[0].astype(F32)) / (den + back[1].astype(F32))

    num, den = _sums(both, both_mats)
    gate_ref[...] = merge(num[:, :256], den[:, :256], gate_back)
    up_ref[...] = merge(num[:, 256:], den[:, 256:], up_back)
    num, den = _sums(down, down_mats)
    down_ref[...] = merge(num, den, down_back)


STEPS = 2


def _rows(height, width, base=0, steps=STEPS):
    return pl.BlockSpec((height // steps, width), lambda i, half_ref: (base + i, 0))


def _pair(height, width, steps=STEPS):
    return pl.BlockSpec((2, height // steps, width), lambda i, half_ref: (0, i, 0))


def _half_rows(height, width, column=0, steps=STEPS):
    return pl.BlockSpec(
        (height // steps, width), lambda i, half_ref: (half_ref[0] * steps + i, column)
    )


def _half_columns(height, width, steps=STEPS):
    return pl.BlockSpec((height // steps, width), lambda i, half_ref: (i, half_ref[0]))


def _call(kernel, half, operands, in_specs, out_shapes, out_specs, steps=STEPS):
    return pl.pallas_call(
        kernel,
        grid_spec=pltpu.PrefetchScalarGridSpec(
            num_scalar_prefetch=1, grid=(steps,), in_specs=in_specs, out_specs=out_specs
        ),
        out_shape=out_shapes,
        cost_estimate=pl.CostEstimate(flops=1, bytes_accessed=1, transcendentals=0),
    )(half, *operands)


def leaving(half, fishers, mats, mat_spec):
    height, width = fishers[0].shape
    return _call(
        _away_kernel,
        half,
        [*fishers, *mats],
        [_rows(height, width)] * 4 + [mat_spec] * 4,
        [jax.ShapeDtypeStruct((2, height, width), BF16)],
        [_pair(height, width)],
    )[0]


def merged(half, owns, both_line, down_line, gate_back, up_back, down_back):
    steps = 4
    return _call(
        _merge_kernel,
        half,
        [*owns, *owns, *both_line, *down_line, gate_back, up_back, down_back],
        [_rows(512, 512, 0, steps)] * 4
        + [_rows(256, 512, 512 // (256 // steps), steps)] * 4
        + [_half_rows(512, 512, 0, steps)] * 4
        + [_half_columns(256, 512, steps)] * 4
        + [_pair(512, 256, steps), _pair(512, 256, steps), _pair(256, 512, steps)],
        [
            jax.ShapeDtypeStruct((512, 256), F32),
            jax.ShapeDtypeStruct((512, 256), F32),
            jax.ShapeDtypeStruct((256, 512), F32),
        ],
        [_rows(512, 256, 0, steps), _rows(512, 256, 0, steps), _rows(256, 512, 0, steps)],
        steps,
    )


def body(inputs, targets, gain, w_gate, w_up, w_down):
    gain_row = gain[0]
    down_mat = w_down[0]
    width = inputs.shape[3]
    scale_model = 1.0 / math.sqrt(width)
    scale_hidden = 1.0 / math.sqrt(w_down.shape[1] * 32)
    core = lax.axis_index("fsdp") % 2
    branch = lax.axis_index("branch")
    y_at, zh_at = branch // 2, branch % 2
    zh_own = jnp.reshape(zh_at, (1,)).astype(jnp.int32)
    zh_away = 1 - zh_own

    def slot_of(by):
        return (y_at + by) % 4

    def slices(mat, axis):
        return [
            lax.dynamic_slice_in_dim(mat, slot_of(by) * 1024, 1024, axis) for by in (0,) + RELATIVE
        ]

    def fetch(part, by):
        return shift(part, "y", by)

    x_pair = pair_up(inputs[0], core)
    down_parts = slices(down_mat, 1)
    down_near = [fetch(part, by) for by, part in zip(RELATIVE, down_parts[1:3])]
    line = gather_line(x_pair)
    line, target_rows, down_far = tie(line, targets[0], down_parts[3])
    target_pair = pair_up(target_rows, core)
    down_far = fetch(down_far, 2)
    last_line, down_near = tie(line, down_near)
    tokens = jnp.stack(
        [line] + [shift(line, "x", by) for by in RELATIVE[:2]] + [shift(last_line, "x", 2)]
    )
    both_mat = jnp.concatenate([w_gate[0], w_up[0]], axis=1)
    tokens, target_pair, down_far, both_mat = tie(tokens, target_pair, down_far, both_mat)
    down_line = [down_parts[0]] + down_near + [down_far]
    both_parts = slices(both_mat, 0)
    near = [fetch(part, by) for by, part in zip(RELATIVE, both_parts[1:3])]
    tokens = [tokens, shift(tokens, "core", 1)]

    def times(left, mat, scale):
        return jnp.einsum("xkmd,df->xkmf", left, mat, preferred_element_type=F32) * scale

    def forward(rows):
        pre = times(rows, both_mat, scale_model)
        gate_pre, up_pre = pre[..., :256], pre[..., 256:]
        hidden = (gate_pre * jax.nn.sigmoid(gate_pre) * up_pre).astype(BF16)
        return pre, hidden, times(hidden, down_mat, scale_hidden).astype(BF16)

    steps = [forward(rows) for rows in tokens]
    hiddens = [step[1] for step in steps]
    chip = (steps[0][2].astype(F32) + shift(steps[1][2], "core", 1).astype(F32)).astype(BF16)
    chip = scatter([chip[i] for i in range(4)], "x")
    chip, far = tie(chip, both_parts[3])
    far = fetch(far, 2)
    parts = [chip[:, 8 * i : 8 * i + 8] for i in range(4)]
    parts[3], near = tie(parts[3], near)
    summed = scatter(parts, "zl")
    out_rows = x_pair.astype(F32) + summed.astype(F32)
    grad_local = norm_grad(out_rows, target_pair.astype(F32), gain_row)
    grads = jnp.stack(gather(gather_line(grad_local), "x"))
    grads, far = tie(grads, far)
    both_line = [both_parts[0]] + near + [far]

    def backward(grad_out, pre):
        grad_hidden = (
            jnp.einsum("xkmd,fd->xkmf", grad_out, down_mat, preferred_element_type=F32)
            * scale_hidden
        )
        gate_pre, up_pre = pre[..., :256], pre[..., 256:]
        sig = jax.nn.sigmoid(gate_pre)
        d_gate = grad_hidden * up_pre * sig * (1.0 + gate_pre * (1.0 - sig))
        return d_gate.astype(BF16), (grad_hidden * gate_pre * sig).astype(BF16)

    other = shift(grads, "core", 1)
    other, d_own = tie(other, backward(grads, steps[0][0]))
    grads = [grads, other]

    def blocks(half, *jobs):
        slots = jnp.concatenate([2 * slot_of(by) + half for by in RELATIVE + (0,)])
        return fisher_blocks(slots, *jobs)

    def exchange(parts):
        return [parts[3]] + [shift(part, "y", by) for by, part in zip(RELATIVE, parts)]

    down_away = blocks(zh_away, (hiddens, grads, scale_hidden, 1))
    grads, down_away = tie(grads, down_away)
    down_away = exchange(down_away)

    d_other = backward(grads[1], steps[1][0])
    d_gates, d_ups = [d_own[0], d_other[0]], [d_own[1], d_other[1]]
    gate_away = blocks(zh_away, (tokens, d_gates, scale_model, 0))

    (down_away, gate_away, hiddens, grads, tokens, d_gates, d_ups) = tie(
        down_away, gate_away, hiddens, grads, tokens, d_gates, d_ups
    )
    down_sent = leaving(zh_away, down_away, down_line, _half_columns(256, 512))
    down_sent, gate_away, tokens, d_ups = tie(down_sent, gate_away, tokens, d_ups)
    down_back = shift(down_sent, "zh", 1)
    gate_away = exchange(gate_away)
    up_away = blocks(zh_away, (tokens, d_ups, scale_model, 0))

    gate_away, up_away, hiddens, grads, tokens, d_gates, d_ups = tie(
        gate_away, up_away, hiddens, grads, tokens, d_gates, d_ups
    )
    gate_sent = leaving(zh_away, gate_away, both_line, _half_rows(512, 256))
    gate_sent, up_away, hiddens, grads, tokens, d_gates, d_ups = tie(
        gate_sent, up_away, hiddens, grads, tokens, d_gates, d_ups
    )
    gate_back = shift(gate_sent, "zh", 1)
    up_away = exchange(up_away)
    d_both = [jnp.concatenate(pair, axis=-1) for pair in zip(d_gates, d_ups)]
    own = blocks(
        zh_own, (tokens, d_both, scale_model, 0), (hiddens, grads, scale_hidden, 1)
    )

    up_away, own, down_back = tie(up_away, own, down_back)
    up_sent = leaving(zh_away, up_away, both_line, _half_rows(512, 256, 1))
    up_sent, own = tie(up_sent, own)
    far_own, gate_back = tie(own[2], gate_back)
    own = [own[0], own[1], far_own, own[3]]
    up_back = shift(up_sent, "zh", 1)
    owns = exchange(own)
    gate, up, down = merged(zh_own, owns, both_line, down_line, gate_back, up_back, down_back)
    return gate, up, down


def solution(mesh):
    placed = (
        P("branch", None, "fsdp", None),
        P("branch", None, "fsdp", None),
        P("branch", None),
        P("branch", None, "fsdp"),
        P("branch", None, "fsdp"),
        P("branch", "fsdp", None),
    )
    return jax.shard_map(
        body,
        mesh=mesh,
        in_specs=placed,
        out_specs=(P("branch", "fsdp"), P("branch", "fsdp"), P("fsdp", "branch")),
        check_vma=False,
    )
```

```python
import functools
import math

import jax
import jax.numpy as jnp
from jax import lax
from jax.experimental import pallas as pl
from jax.experimental.pallas import tpu as pltpu
from jax.sharding import PartitionSpec as P

F32 = jnp.float32
BF16 = jnp.bfloat16

SIZES = {"branch": (("y", 4), ("zh", 2)), "fsdp": (("x", 4), ("zl", 4), ("core", 2))}


def _ring(axis, name, shift):
    parts = SIZES[axis]
    total = math.prod(size for _, size in parts)
    stride = 1
    for part, size in reversed(parts):
        if part == name:
            break
        stride *= size
    pairs = []
    for i in range(total):
        at = (i // stride) % size
        pairs.append((i, i + ((at + shift) % size - at) * stride))
    return pairs


def shift(value, name, by):
    axis = "branch" if name in ("y", "zh") else "fsdp"
    return lax.ppermute(value, axis, _ring(axis, name, by))


RELATIVE = (1, 3, 2)


def tie(*values):
    return lax.optimization_barrier(values)


def gather(value, name):
    return [value] + [shift(value, name, by) for by in RELATIVE]


def scatter(parts, name):
    back = [shift(part, name, -by) for by, part in zip(RELATIVE, parts[1:])]
    total = parts[0].astype(F32)
    for piece in back:
        total = total + piece.astype(F32)
    return total.astype(BF16)


def gather_line(rows):
    return jnp.concatenate(gather(rows, "zl"), axis=1)


def pair_up(rows, core):
    mine = lax.dynamic_slice_in_dim(rows, 2 * core, 2, 0)
    theirs = lax.dynamic_slice_in_dim(rows, 2 - 2 * core, 2, 0)
    return lax.optimization_barrier(
        jnp.concatenate([mine, shift(theirs, "core", 1)], axis=1)
    )


def norm_grad(out_rows, target_rows, gain_row):
    recip = lax.rsqrt(jnp.mean(out_rows * out_rows, axis=-1, keepdims=True) + 1e-05)
    normed = out_rows * recip * gain_row
    delta = normed - target_rows
    center = jnp.mean(delta * gain_row * out_rows, axis=-1, keepdims=True)
    return (gain_row * recip * delta - recip * recip * recip * out_rows * center).astype(BF16)


def _fisher_kernel(slots_ref, *refs, jobs, count, tile):
    del slots_ref
    ins, outs = refs[:-count], refs[-count:]

    def rows(ref, item, at=None):
        piece = ref[:, item] if at is None else ref[:, item, :, at : at + tile]
        return piece.reshape(piece.shape[0] * piece.shape[1], piece.shape[2])

    for at_out, out_ref in enumerate(outs):

        @pl.when(pl.program_id(0) == at_out)
        def _(out_ref=out_ref):
            base = 0
            for job, factor in enumerate(jobs):
                lefts, rights = ins[4 * job : 4 * job + 2], ins[4 * job + 2 : 4 * job + 4]
                height = lefts[0].shape[3]
                for at in range(0, height, tile):
                    total = None
                    for left_ref, right_ref in zip(lefts, rights):
                        for item in range(left_ref.shape[1]):
                            grad = lax.dot_general(
                                rows(left_ref, item, at),
                                rows(right_ref, item),
                                (((0,), (0,)), ((), ())),
                                preferred_element_type=F32,
                            )
                            total = grad * grad if total is None else total + grad * grad
                    out_ref[base + at : base + at + tile, :] = (total * factor).astype(BF16)
                base += height


def fisher_blocks(slots, *jobs):
    count = slots.shape[0]
    specs, operands, factors = [], [], []
    height, width = 0, 0
    for lefts, rights, scale, wide in jobs:
        lead = lefts[0].shape[:3]
        cut = pl.BlockSpec(lead + (512,), lambda i, slots_ref: (0, 0, 0, slots_ref[i]))
        held = pl.BlockSpec((lefts if wide else rights)[0].shape, lambda i, slots_ref: (0, 0, 0, 0))
        specs += [held, held, cut, cut] if wide else [cut, cut, held, held]
        operands += [*lefts, *rights]
        factors.append(scale * scale / 4)
        height += lefts[0].shape[3] if wide else 512
        width = 512 if wide else rights[0].shape[3]
    out_shape = (height, width)
    return pl.pallas_call(
        functools.partial(_fisher_kernel, jobs=tuple(factors), count=count, tile=256),
        grid_spec=pltpu.PrefetchScalarGridSpec(
            num_scalar_prefetch=1,
            grid=(count,),
            in_specs=specs,
            out_specs=[pl.BlockSpec(out_shape, lambda i, slots_ref: (0, 0))] * count,
        ),
        out_shape=[jax.ShapeDtypeStruct(out_shape, BF16)] * count,
        compiler_params=pltpu.CompilerParams(vmem_limit_bytes=48 * 1024 * 1024),
        cost_estimate=pl.CostEstimate(flops=1, bytes_accessed=1, transcendentals=0),
    )(slots, *operands)


def _sums(fisher_refs, mat_refs):
    num, den = 0.0, 0.0
    for fisher_ref, mat_ref in zip(fisher_refs, mat_refs):
        part = fisher_ref[...].astype(F32)
        num = num + part * mat_ref[...].astype(F32)
        den = den + part
    return num, den


def _away_kernel(half_ref, *refs):
    del half_ref
    num, den = _sums(refs[:4], refs[4:8])
    refs[8][0] = num.astype(BF16)
    refs[8][1] = den.astype(BF16)


def _merge_kernel(half_ref, *refs):
    del half_ref
    both, down, both_mats, down_mats = (refs[4 * i : 4 * i + 4] for i in range(4))
    gate_back, up_back, down_back, gate_ref, up_ref, down_ref = refs[16:]

    def merge(num, den, back):
        return (num + back[0].astype(F32)) / (den + back[1].astype(F32))

    num, den = _sums(both, both_mats)
    gate_ref[...] = merge(num[:, :256], den[:, :256], gate_back)
    up_ref[...] = merge(num[:, 256:], den[:, 256:], up_back)
    num, den = _sums(down, down_mats)
    down_ref[...] = merge(num, den, down_back)


STEPS = 2


def _rows(height, width, base=0, steps=STEPS):
    return pl.BlockSpec((height // steps, width), lambda i, half_ref: (base + i, 0))


def _pair(height, width, steps=STEPS):
    return pl.BlockSpec((2, height // steps, width), lambda i, half_ref: (0, i, 0))


def _half_rows(height, width, column=0, steps=STEPS):
    return pl.BlockSpec(
        (height // steps, width), lambda i, half_ref: (half_ref[0] * steps + i, column)
    )


def _half_columns(height, width, steps=STEPS):
    return pl.BlockSpec((height // steps, width), lambda i, half_ref: (i, half_ref[0]))


def _call(kernel, half, operands, in_specs, out_shapes, out_specs, steps=STEPS):
    return pl.pallas_call(
        kernel,
        grid_spec=pltpu.PrefetchScalarGridSpec(
            num_scalar_prefetch=1, grid=(steps,), in_specs=in_specs, out_specs=out_specs
        ),
        out_shape=out_shapes,
        cost_estimate=pl.CostEstimate(flops=1, bytes_accessed=1, transcendentals=0),
    )(half, *operands)


def leaving(half, fishers, mats, mat_spec):
    height, width = fishers[0].shape
    return _call(
        _away_kernel,
        half,
        [*fishers, *mats],
        [_rows(height, width)] * 4 + [mat_spec] * 4,
        [jax.ShapeDtypeStruct((2, height, width), BF16)],
        [_pair(height, width)],
    )[0]


def merged(half, near, both_far, down_far, both_line, down_line, gate_back, up_back, down_back):
    steps = 2
    return _call(
        _merge_kernel,
        half,
        [*near, both_far, *near, down_far, *both_line, *down_line, gate_back, up_back, down_back],
        [_rows(512, 512, 0, steps)] * 4
        + [_rows(256, 512, 512 // (256 // steps), steps)] * 3
        + [_rows(256, 512, 0, steps)]
        + [_half_rows(512, 512, 0, steps)] * 4
        + [_half_columns(256, 512, steps)] * 4
        + [_pair(512, 256, steps), _pair(512, 256, steps), _pair(256, 512, steps)],
        [
            jax.ShapeDtypeStruct((512, 256), F32),
            jax.ShapeDtypeStruct((512, 256), F32),
            jax.ShapeDtypeStruct((256, 512), F32),
        ],
        [_rows(512, 256, 0, steps), _rows(512, 256, 0, steps), _rows(256, 512, 0, steps)],
        steps,
    )


def body(inputs, targets, gain, w_gate, w_up, w_down):
    gain_row = gain[0]
    down_mat = w_down[0]
    width = inputs.shape[3]
    scale_model = 1.0 / math.sqrt(width)
    scale_hidden = 1.0 / math.sqrt(w_down.shape[1] * 32)
    core = lax.axis_index("fsdp") % 2
    branch = lax.axis_index("branch")
    y_at, zh_at = branch // 2, branch % 2
    zh_own = jnp.reshape(zh_at, (1,)).astype(jnp.int32)
    zh_away = 1 - zh_own

    def slot_of(by):
        return (y_at + by) % 4

    def slices(mat, axis):
        return [
            lax.dynamic_slice_in_dim(mat, slot_of(by) * 1024, 1024, axis) for by in (0,) + RELATIVE
        ]

    def fetch(part, by):
        return shift(part, "y", by)

    x_pair = pair_up(inputs[0], core)
    down_parts = slices(down_mat, 1)
    down_near = [fetch(part, by) for by, part in zip(RELATIVE, down_parts[1:3])]
    line = gather_line(x_pair)
    line, target_rows, down_far = tie(line, targets[0], down_parts[3])
    target_pair = pair_up(target_rows, core)
    down_far = fetch(down_far, 2)
    last_line, down_near = tie(line, down_near)
    tokens = jnp.stack(
        [line] + [shift(last_line if by == 1 else line, "x", by) for by in RELATIVE]
    )
    both_mat = jnp.concatenate([w_gate[0], w_up[0]], axis=1)
    tokens, target_pair, down_far, both_mat = tie(tokens, target_pair, down_far, both_mat)
    down_line = [down_parts[0]] + down_near + [down_far]
    both_parts = slices(both_mat, 0)
    near = [fetch(part, by) for by, part in zip(RELATIVE, both_parts[1:3])]
    tokens = [tokens, shift(tokens, "core", 1)]

    def times(left, mat, scale):
        return jnp.einsum("xkmd,df->xkmf", left, mat, preferred_element_type=F32) * scale

    def forward(rows):
        pre = times(rows, both_mat, scale_model)
        gate_pre, up_pre = pre[..., :256], pre[..., 256:]
        hidden = (gate_pre * jax.nn.sigmoid(gate_pre) * up_pre).astype(BF16)
        return pre, hidden, times(hidden, down_mat, scale_hidden).astype(BF16)

    steps = [forward(rows) for rows in tokens]
    hiddens = [step[1] for step in steps]
    chip = (steps[0][2].astype(F32) + shift(steps[1][2], "core", 1).astype(F32)).astype(BF16)
    chip = scatter([chip[i] for i in range(4)], "x")
    chip, far = tie(chip, both_parts[3])
    far = fetch(far, 2)
    parts = [chip[:, 8 * i : 8 * i + 8] for i in range(4)]
    parts[1], near = tie(parts[1], near)
    summed = scatter(parts, "zl")
    out_rows = x_pair.astype(F32) + summed.astype(F32)
    grad_local = norm_grad(out_rows, target_pair.astype(F32), gain_row)
    grads = jnp.stack(gather(gather_line(grad_local), "x"))
    grads, far = tie(grads, far)
    both_line = [both_parts[0]] + near + [far]

    def backward(grad_out, pre):
        grad_hidden = (
            jnp.einsum("xkmd,fd->xkmf", grad_out, down_mat, preferred_element_type=F32)
            * scale_hidden
        )
        gate_pre, up_pre = pre[..., :256], pre[..., 256:]
        sig = jax.nn.sigmoid(gate_pre)
        d_gate = grad_hidden * up_pre * sig * (1.0 + gate_pre * (1.0 - sig))
        return d_gate.astype(BF16), (grad_hidden * gate_pre * sig).astype(BF16)

    other = shift(grads, "core", 1)
    other, d_own = tie(other, backward(grads, steps[0][0]))
    grads = [grads, other]

    def blocks(half, *jobs):
        slots = jnp.concatenate([2 * slot_of(by) + half for by in RELATIVE + (0,)])
        return fisher_blocks(slots, *jobs)

    def exchange(parts):
        return [parts[3]] + [shift(part, "y", by) for by, part in zip(RELATIVE, parts)]

    down_away = blocks(zh_away, (hiddens, grads, scale_hidden, 1))
    grads, down_away = tie(grads, down_away)
    down_away = exchange(down_away)

    d_other = backward(grads[1], steps[1][0])
    d_gates, d_ups = [d_own[0], d_other[0]], [d_own[1], d_other[1]]
    gate_away = blocks(zh_away, (tokens, d_gates, scale_model, 0))

    near_away, gate_away, hiddens, grads, tokens, d_gates, d_ups = tie(
        down_away[1:3], gate_away, hiddens, grads, tokens, d_gates, d_ups
    )
    gate_away = exchange(gate_away)
    down_sent = leaving(
        zh_away, [down_away[0], *near_away, down_away[3]], down_line, _half_columns(256, 512)
    )
    down_sent, tokens, d_ups = tie(down_sent, tokens, d_ups)
    down_back = shift(down_sent, "zh", 1)
    up_away = blocks(zh_away, (tokens, d_ups, scale_model, 0))

    near_away, up_away, hiddens, grads, tokens, d_gates, d_ups = tie(
        gate_away[1:3], up_away, hiddens, grads, tokens, d_gates, d_ups
    )
    up_away = exchange(up_away)
    gate_sent = leaving(
        zh_away, [gate_away[0], *near_away, gate_away[3]], both_line, _half_rows(512, 256)
    )
    gate_sent, hiddens, grads, tokens, d_gates, d_ups = tie(
        gate_sent, hiddens, grads, tokens, d_gates, d_ups
    )
    gate_back = shift(gate_sent, "zh", 1)
    d_both = [jnp.concatenate(pair, axis=-1) for pair in zip(d_gates, d_ups)]
    own = blocks(
        zh_own, (tokens, d_both, scale_model, 0), (hiddens, grads, scale_hidden, 1)
    )

    up_away, own, down_back = tie(up_away, own, down_back)
    up_sent = leaving(zh_away, up_away, both_line, _half_rows(512, 256, 1))
    up_sent, own = tie(up_sent, own)
    last_own, gate_back = tie(own[2][512:], gate_back)
    both_far, down_far = shift(own[2][:512], "y", 2), shift(last_own, "y", 2)
    up_back = shift(up_sent, "zh", 1)
    near_own = [own[3]] + [shift(part, "y", by) for by, part in zip(RELATIVE, own[:2])]
    gate, up, down = merged(zh_own, near_own, both_far, down_far, both_line, down_line, gate_back, up_back, down_back)
    return gate, up, down


def solution(mesh):
    placed = (
        P("branch", None, "fsdp", None),
        P("branch", None, "fsdp", None),
        P("branch", None),
        P("branch", None, "fsdp"),
        P("branch", None, "fsdp"),
        P("branch", "fsdp", None),
    )
    return jax.shard_map(
        body,
        mesh=mesh,
        in_specs=placed,
        out_specs=(P("branch", "fsdp"), P("branch", "fsdp"), P("fsdp", "branch")),
        check_vma=False,
    )
```

```python
import functools
import math

import jax
import jax.numpy as jnp
from jax import lax
from jax.experimental import pallas as pl
from jax.experimental.pallas import tpu as pltpu
from jax.sharding import PartitionSpec as P

F32 = jnp.float32
BF16 = jnp.bfloat16

SIZES = {"branch": (("y", 4), ("zh", 2)), "fsdp": (("x", 4), ("zl", 4), ("core", 2))}


def _ring(axis, name, shift):
    parts = SIZES[axis]
    total = math.prod(size for _, size in parts)
    stride = 1
    for part, size in reversed(parts):
        if part == name:
            break
        stride *= size
    pairs = []
    for i in range(total):
        at = (i // stride) % size
        pairs.append((i, i + ((at + shift) % size - at) * stride))
    return pairs


def shift(value, name, by):
    axis = "branch" if name in ("y", "zh") else "fsdp"
    return lax.ppermute(value, axis, _ring(axis, name, by))


RELATIVE = (1, 3, 2)


def tie(*values):
    return lax.optimization_barrier(values)


def gather(value, name):
    return [value] + [shift(value, name, by) for by in RELATIVE]


def scatter(parts, name):
    back = [shift(part, name, -by) for by, part in zip(RELATIVE, parts[1:])]
    total = parts[0].astype(F32)
    for piece in back:
        total = total + piece.astype(F32)
    return total.astype(BF16)


def gather_line(rows):
    return jnp.concatenate(gather(rows, "zl"), axis=1)


def pair_up(rows, core):
    mine = lax.dynamic_slice_in_dim(rows, 2 * core, 2, 0)
    theirs = lax.dynamic_slice_in_dim(rows, 2 - 2 * core, 2, 0)
    return lax.optimization_barrier(
        jnp.concatenate([mine, shift(theirs, "core", 1)], axis=1)
    )


def norm_grad(out_rows, target_rows, gain_row):
    recip = lax.rsqrt(jnp.mean(out_rows * out_rows, axis=-1, keepdims=True) + 1e-05)
    normed = out_rows * recip * gain_row
    delta = normed - target_rows
    center = jnp.mean(delta * gain_row * out_rows, axis=-1, keepdims=True)
    return (gain_row * recip * delta - recip * recip * recip * out_rows * center).astype(BF16)


def _fisher_kernel(slots_ref, *refs, jobs, count, tile):
    del slots_ref
    ins, outs = refs[:-count], refs[-count:]

    def rows(ref, item, at=None):
        piece = ref[:, item] if at is None else ref[:, item, :, at : at + tile]
        return piece.reshape(piece.shape[0] * piece.shape[1], piece.shape[2])

    for at_out, out_ref in enumerate(outs):

        @pl.when(pl.program_id(0) == at_out)
        def _(out_ref=out_ref):
            base = 0
            for job, factor in enumerate(jobs):
                lefts, rights = ins[4 * job : 4 * job + 2], ins[4 * job + 2 : 4 * job + 4]
                height = lefts[0].shape[3]
                for at in range(0, height, tile):
                    total = None
                    for left_ref, right_ref in zip(lefts, rights):
                        for item in range(left_ref.shape[1]):
                            grad = lax.dot_general(
                                rows(left_ref, item, at),
                                rows(right_ref, item),
                                (((0,), (0,)), ((), ())),
                                preferred_element_type=F32,
                            )
                            total = grad * grad if total is None else total + grad * grad
                    out_ref[base + at : base + at + tile, :] = (total * factor).astype(BF16)
                base += height


def fisher_blocks(slots, *jobs):
    count = slots.shape[0]
    specs, operands, factors = [], [], []
    height, width = 0, 0
    for lefts, rights, scale, wide in jobs:
        lead = lefts[0].shape[:3]
        cut = pl.BlockSpec(lead + (512,), lambda i, slots_ref: (0, 0, 0, slots_ref[i]))
        held = pl.BlockSpec((lefts if wide else rights)[0].shape, lambda i, slots_ref: (0, 0, 0, 0))
        specs += [held, held, cut, cut] if wide else [cut, cut, held, held]
        operands += [*lefts, *rights]
        factors.append(scale * scale / 4)
        height += lefts[0].shape[3] if wide else 512
        width = 512 if wide else rights[0].shape[3]
    out_shape = (height, width)
    return pl.pallas_call(
        functools.partial(_fisher_kernel, jobs=tuple(factors), count=count, tile=256),
        grid_spec=pltpu.PrefetchScalarGridSpec(
            num_scalar_prefetch=1,
            grid=(count,),
            in_specs=specs,
            out_specs=[pl.BlockSpec(out_shape, lambda i, slots_ref: (0, 0))] * count,
        ),
        out_shape=[jax.ShapeDtypeStruct(out_shape, BF16)] * count,
        compiler_params=pltpu.CompilerParams(vmem_limit_bytes=48 * 1024 * 1024),
        cost_estimate=pl.CostEstimate(flops=1, bytes_accessed=1, transcendentals=0),
    )(slots, *operands)


def _sums(fisher_refs, mat_refs):
    num, den = 0.0, 0.0
    for fisher_ref, mat_ref in zip(fisher_refs, mat_refs):
        part = fisher_ref[...].astype(F32)
        num = num + part * mat_ref[...].astype(F32)
        den = den + part
    return num, den


def _away_kernel(half_ref, *refs):
    del half_ref
    num, den = _sums(refs[:4], refs[4:8])
    refs[8][0] = num.astype(BF16)
    refs[8][1] = den.astype(BF16)


def _merge_kernel(half_ref, *refs):
    del half_ref
    both, down, both_mats, down_mats = (refs[4 * i : 4 * i + 4] for i in range(4))
    gate_back, up_back, down_back, gate_ref, up_ref, down_ref = refs[16:]

    def merge(num, den, back):
        return (num + back[0].astype(F32)) / (den + back[1].astype(F32))

    num, den = _sums(both, both_mats)
    gate_ref[...] = merge(num[:, :256], den[:, :256], gate_back)
    up_ref[...] = merge(num[:, 256:], den[:, 256:], up_back)
    num, den = _sums(down, down_mats)
    down_ref[...] = merge(num, den, down_back)


STEPS = 2


def _rows(height, width, base=0, steps=STEPS):
    return pl.BlockSpec((height // steps, width), lambda i, half_ref: (base + i, 0))


def _pair(height, width, steps=STEPS):
    return pl.BlockSpec((2, height // steps, width), lambda i, half_ref: (0, i, 0))


def _half_rows(height, width, column=0, steps=STEPS):
    return pl.BlockSpec(
        (height // steps, width), lambda i, half_ref: (half_ref[0] * steps + i, column)
    )


def _half_columns(height, width, steps=STEPS):
    return pl.BlockSpec((height // steps, width), lambda i, half_ref: (i, half_ref[0]))


def _call(kernel, half, operands, in_specs, out_shapes, out_specs, steps=STEPS):
    return pl.pallas_call(
        kernel,
        grid_spec=pltpu.PrefetchScalarGridSpec(
            num_scalar_prefetch=1, grid=(steps,), in_specs=in_specs, out_specs=out_specs
        ),
        out_shape=out_shapes,
        cost_estimate=pl.CostEstimate(flops=1, bytes_accessed=1, transcendentals=0),
    )(half, *operands)


def leaving(half, fishers, mats, mat_spec):
    height, width = fishers[0].shape
    return _call(
        _away_kernel,
        half,
        [*fishers, *mats],
        [_rows(height, width)] * 4 + [mat_spec] * 4,
        [jax.ShapeDtypeStruct((2, height, width), BF16)],
        [_pair(height, width)],
    )[0]


def merged(half, near, both_far, down_far, both_line, down_line, gate_back, up_back, down_back):
    steps = 2
    return _call(
        _merge_kernel,
        half,
        [*near, both_far, *near, down_far, *both_line, *down_line, gate_back, up_back, down_back],
        [_rows(512, 512, 0, steps)] * 4
        + [_rows(256, 512, 512 // (256 // steps), steps)] * 3
        + [_rows(256, 512, 0, steps)]
        + [_half_rows(512, 512, 0, steps)] * 4
        + [_half_columns(256, 512, steps)] * 4
        + [_pair(512, 256, steps), _pair(512, 256, steps), _pair(256, 512, steps)],
        [
            jax.ShapeDtypeStruct((512, 256), F32),
            jax.ShapeDtypeStruct((512, 256), F32),
            jax.ShapeDtypeStruct((256, 512), F32),
        ],
        [_rows(512, 256, 0, steps), _rows(512, 256, 0, steps), _rows(256, 512, 0, steps)],
        steps,
    )


def body(inputs, targets, gain, w_gate, w_up, w_down):
    gain_row = gain[0]
    down_mat = w_down[0]
    width = inputs.shape[3]
    scale_model = 1.0 / math.sqrt(width)
    scale_hidden = 1.0 / math.sqrt(w_down.shape[1] * 32)
    core = lax.axis_index("fsdp") % 2
    branch = lax.axis_index("branch")
    y_at, zh_at = branch // 2, branch % 2
    zh_own = jnp.reshape(zh_at, (1,)).astype(jnp.int32)
    zh_away = 1 - zh_own

    def slot_of(by):
        return (y_at + by) % 4

    def slices(mat, axis):
        return [
            lax.dynamic_slice_in_dim(mat, slot_of(by) * 1024, 1024, axis) for by in (0,) + RELATIVE
        ]

    def fetch(part, by):
        return shift(part, "y", by)

    x_pair = pair_up(inputs[0], core)
    down_parts = slices(down_mat, 1)
    down_near = [fetch(part, by) for by, part in zip(RELATIVE, down_parts[1:3])]
    line = gather_line(x_pair)
    line, target_rows, down_far = tie(line, targets[0], down_parts[3])
    target_pair = pair_up(target_rows, core)
    down_far = fetch(down_far, 2)
    last_line, down_near = tie(line, down_near)
    tokens = jnp.stack(
        [line] + [shift(last_line if by == 1 else line, "x", by) for by in RELATIVE]
    )
    both_mat = jnp.concatenate([w_gate[0], w_up[0]], axis=1)
    tokens, target_pair, down_far, both_mat = tie(tokens, target_pair, down_far, both_mat)
    down_line = [down_parts[0]] + down_near + [down_far]
    both_parts = slices(both_mat, 0)
    near = [fetch(part, by) for by, part in zip(RELATIVE, both_parts[1:3])]
    tokens = [tokens, shift(tokens, "core", 1)]

    def times(left, mat, scale):
        return jnp.einsum("xkmd,df->xkmf", left, mat, preferred_element_type=F32) * scale

    def forward(rows):
        pre = times(rows, both_mat, scale_model)
        gate_pre, up_pre = pre[..., :256], pre[..., 256:]
        hidden = (gate_pre * jax.nn.sigmoid(gate_pre) * up_pre).astype(BF16)
        return pre, hidden, times(hidden, down_mat, scale_hidden).astype(BF16)

    steps = [forward(rows) for rows in tokens]
    hiddens = [step[1] for step in steps]
    chip = (steps[0][2].astype(F32) + shift(steps[1][2], "core", 1).astype(F32)).astype(BF16)
    chip = scatter([chip[i] for i in range(4)], "x")
    chip, far = tie(chip, both_parts[3])
    far = fetch(far, 2)
    parts = [chip[:, 8 * i : 8 * i + 8] for i in range(4)]
    parts[1], near = tie(parts[1], near)
    summed = scatter(parts, "zl")
    out_rows = x_pair.astype(F32) + summed.astype(F32)
    grad_local = norm_grad(out_rows, target_pair.astype(F32), gain_row)
    grads = jnp.zeros((4,) + line.shape, BF16)
    for i, piece in enumerate(gather(gather_line(grad_local), "x")):
        grads = lax.dynamic_update_index_in_dim(grads, piece, i, 0)
    grads, far = tie(grads, far)
    both_line = [both_parts[0]] + near + [far]

    def backward(grad_out, pre):
        grad_hidden = (
            jnp.einsum("xkmd,fd->xkmf", grad_out, down_mat, preferred_element_type=F32)
            * scale_hidden
        )
        gate_pre, up_pre = pre[..., :256], pre[..., 256:]
        sig = jax.nn.sigmoid(gate_pre)
        d_gate = grad_hidden * up_pre * sig * (1.0 + gate_pre * (1.0 - sig))
        return d_gate.astype(BF16), (grad_hidden * gate_pre * sig).astype(BF16)

    other = shift(grads, "core", 1)
    other, d_own = tie(other, backward(grads, steps[0][0]))
    grads = [grads, other]

    def blocks(half, *jobs):
        slots = jnp.concatenate([2 * slot_of(by) + half for by in RELATIVE + (0,)])
        return fisher_blocks(slots, *jobs)

    def exchange(parts):
        return [parts[3]] + [shift(part, "y", by) for by, part in zip(RELATIVE, parts)]

    down_away = blocks(zh_away, (hiddens, grads, scale_hidden, 1))
    grads, down_away = tie(grads, down_away)
    down_away = exchange(down_away)

    d_other = backward(grads[1], steps[1][0])
    d_gates, d_ups = [d_own[0], d_other[0]], [d_own[1], d_other[1]]
    gate_away = blocks(zh_away, (tokens, d_gates, scale_model, 0))

    near_away, gate_away, hiddens, grads, tokens, d_gates, d_ups = tie(
        down_away[1:3], gate_away, hiddens, grads, tokens, d_gates, d_ups
    )
    gate_away = exchange(gate_away)
    down_sent = leaving(
        zh_away, [down_away[0], *near_away, down_away[3]], down_line, _half_columns(256, 512)
    )
    down_sent, tokens, d_ups = tie(down_sent, tokens, d_ups)
    down_back = shift(down_sent, "zh", 1)
    up_away = blocks(zh_away, (tokens, d_ups, scale_model, 0))

    near_away, up_away, hiddens, grads, tokens, d_gates, d_ups = tie(
        gate_away[1:3], up_away, hiddens, grads, tokens, d_gates, d_ups
    )
    up_away = exchange(up_away)
    gate_sent = leaving(
        zh_away, [gate_away[0], *near_away, gate_away[3]], both_line, _half_rows(512, 256)
    )
    gate_sent, hiddens, grads, tokens, d_gates, d_ups = tie(
        gate_sent, hiddens, grads, tokens, d_gates, d_ups
    )
    gate_back = shift(gate_sent, "zh", 1)
    d_both = [jnp.concatenate(pair, axis=-1) for pair in zip(d_gates, d_ups)]
    own = blocks(
        zh_own, (tokens, d_both, scale_model, 0), (hiddens, grads, scale_hidden, 1)
    )

    up_away, own, down_back = tie(up_away, own, down_back)
    up_sent = leaving(zh_away, up_away, both_line, _half_rows(512, 256, 1))
    up_sent, own = tie(up_sent, own)
    last_own, gate_back = tie(own[2][512:], gate_back)
    both_far, down_far = shift(own[2][:512], "y", 2), shift(last_own, "y", 2)
    up_back = shift(up_sent, "zh", 1)
    near_own = [own[3]] + [shift(part, "y", by) for by, part in zip(RELATIVE, own[:2])]
    gate, up, down = merged(zh_own, near_own, both_far, down_far, both_line, down_line, gate_back, up_back, down_back)
    return gate, up, down


def solution(mesh):
    placed = (
        P("branch", None, "fsdp", None),
        P("branch", None, "fsdp", None),
        P("branch", None),
        P("branch", None, "fsdp"),
        P("branch", None, "fsdp"),
        P("branch", "fsdp", None),
    )
    return jax.shard_map(
        body,
        mesh=mesh,
        in_specs=placed,
        out_specs=(P("branch", "fsdp"), P("branch", "fsdp"), P("fsdp", "branch")),
        check_vma=False,
    )
```

```python
import functools
import math

import jax
import jax.numpy as jnp
from jax import lax
from jax.experimental import pallas as pl
from jax.experimental.pallas import tpu as pltpu
from jax.sharding import PartitionSpec as P

F32 = jnp.float32
BF16 = jnp.bfloat16

SIZES = {"branch": (("y", 4), ("zh", 2)), "fsdp": (("x", 4), ("zl", 4), ("core", 2))}


def _ring(axis, name, shift):
    parts = SIZES[axis]
    total = math.prod(size for _, size in parts)
    stride = 1
    for part, size in reversed(parts):
        if part == name:
            break
        stride *= size
    pairs = []
    for i in range(total):
        at = (i // stride) % size
        pairs.append((i, i + ((at + shift) % size - at) * stride))
    return pairs


def shift(value, name, by):
    axis = "branch" if name in ("y", "zh") else "fsdp"
    return lax.ppermute(value, axis, _ring(axis, name, by))


RELATIVE = (1, 3, 2)


def tie(*values):
    return lax.optimization_barrier(values)


def gather(value, name):
    return [value] + [shift(value, name, by) for by in RELATIVE]


def scatter(parts, name):
    back = [shift(part, name, -by) for by, part in zip(RELATIVE, parts[1:])]
    total = parts[0].astype(F32)
    for piece in back:
        total = total + piece.astype(F32)
    return total.astype(BF16)


def gather_line(rows):
    return jnp.concatenate(gather(rows, "zl"), axis=1)


def pair_up(rows, core):
    mine = lax.dynamic_slice_in_dim(rows, 2 * core, 2, 0)
    theirs = lax.dynamic_slice_in_dim(rows, 2 - 2 * core, 2, 0)
    return lax.optimization_barrier(
        jnp.concatenate([mine, shift(theirs, "core", 1)], axis=1)
    )


def norm_grad(out_rows, target_rows, gain_row):
    recip = lax.rsqrt(jnp.mean(out_rows * out_rows, axis=-1, keepdims=True) + 1e-05)
    normed = out_rows * recip * gain_row
    delta = normed - target_rows
    center = jnp.mean(delta * gain_row * out_rows, axis=-1, keepdims=True)
    return (gain_row * recip * delta - recip * recip * recip * out_rows * center).astype(BF16)


def _fisher_kernel(slots_ref, *refs, jobs, count, tile):
    del slots_ref
    ins, outs = refs[:-count], refs[-count:]

    def rows(ref, item, at=None):
        piece = ref[:, item] if at is None else ref[:, item, :, at : at + tile]
        return piece.reshape(piece.shape[0] * piece.shape[1], piece.shape[2])

    for at_out, out_ref in enumerate(outs):

        @pl.when(pl.program_id(0) == at_out)
        def _(out_ref=out_ref):
            base = 0
            for job, factor in enumerate(jobs):
                lefts, rights = ins[4 * job : 4 * job + 2], ins[4 * job + 2 : 4 * job + 4]
                height = lefts[0].shape[3]
                for at in range(0, height, tile):
                    total = None
                    for left_ref, right_ref in zip(lefts, rights):
                        for item in range(left_ref.shape[1]):
                            grad = lax.dot_general(
                                rows(left_ref, item, at),
                                rows(right_ref, item),
                                (((0,), (0,)), ((), ())),
                                preferred_element_type=F32,
                            )
                            total = grad * grad if total is None else total + grad * grad
                    out_ref[base + at : base + at + tile, :] = (total * factor).astype(BF16)
                base += height


def fisher_blocks(slots, *jobs):
    count = slots.shape[0]
    specs, operands, factors = [], [], []
    height, width = 0, 0
    for lefts, rights, scale, wide in jobs:
        lead = lefts[0].shape[:3]
        cut = pl.BlockSpec(lead + (512,), lambda i, slots_ref: (0, 0, 0, slots_ref[i]))
        held = pl.BlockSpec((lefts if wide else rights)[0].shape, lambda i, slots_ref: (0, 0, 0, 0))
        specs += [held, held, cut, cut] if wide else [cut, cut, held, held]
        operands += [*lefts, *rights]
        factors.append(scale * scale / 4)
        height += lefts[0].shape[3] if wide else 512
        width = 512 if wide else rights[0].shape[3]
    out_shape = (height, width)
    return pl.pallas_call(
        functools.partial(_fisher_kernel, jobs=tuple(factors), count=count, tile=256),
        grid_spec=pltpu.PrefetchScalarGridSpec(
            num_scalar_prefetch=1,
            grid=(count,),
            in_specs=specs,
            out_specs=[pl.BlockSpec(out_shape, lambda i, slots_ref: (0, 0))] * count,
        ),
        out_shape=[jax.ShapeDtypeStruct(out_shape, BF16)] * count,
        compiler_params=pltpu.CompilerParams(vmem_limit_bytes=48 * 1024 * 1024),
        cost_estimate=pl.CostEstimate(flops=1, bytes_accessed=1, transcendentals=0),
    )(slots, *operands)


def _sums(fisher_refs, mat_refs):
    num, den = 0.0, 0.0
    for fisher_ref, mat_ref in zip(fisher_refs, mat_refs):
        part = fisher_ref[...].astype(F32)
        num = num + part * mat_ref[...].astype(F32)
        den = den + part
    return num, den


def _away_kernel(half_ref, *refs):
    del half_ref
    num, den = _sums(refs[:4], refs[4:8])
    refs[8][0] = num.astype(BF16)
    refs[8][1] = den.astype(BF16)


def _merge_kernel(half_ref, *refs):
    del half_ref
    both, down, both_mats, down_mats = (refs[4 * i : 4 * i + 4] for i in range(4))
    gate_back, up_back, down_back, gate_ref, up_ref, down_ref = refs[16:]

    def merge(num, den, back):
        return (num + back[0].astype(F32)) / (den + back[1].astype(F32))

    num, den = _sums(both, both_mats)
    gate_ref[...] = merge(num[:, :256], den[:, :256], gate_back)
    up_ref[...] = merge(num[:, 256:], den[:, 256:], up_back)
    num, den = _sums(down, down_mats)
    down_ref[...] = merge(num, den, down_back)


STEPS = 2


def _rows(height, width, base=0, steps=STEPS):
    return pl.BlockSpec((height // steps, width), lambda i, half_ref: (base + i, 0))


def _pair(height, width, steps=STEPS):
    return pl.BlockSpec((2, height // steps, width), lambda i, half_ref: (0, i, 0))


def _half_rows(height, width, column=0, steps=STEPS):
    return pl.BlockSpec(
        (height // steps, width), lambda i, half_ref: (half_ref[0] * steps + i, column)
    )


def _half_columns(height, width, steps=STEPS):
    return pl.BlockSpec((height // steps, width), lambda i, half_ref: (i, half_ref[0]))


def _call(kernel, half, operands, in_specs, out_shapes, out_specs, steps=STEPS):
    return pl.pallas_call(
        kernel,
        grid_spec=pltpu.PrefetchScalarGridSpec(
            num_scalar_prefetch=1, grid=(steps,), in_specs=in_specs, out_specs=out_specs
        ),
        out_shape=out_shapes,
        cost_estimate=pl.CostEstimate(flops=1, bytes_accessed=1, transcendentals=0),
    )(half, *operands)


def leaving(half, fishers, mats, mat_spec):
    height, width = fishers[0].shape
    return _call(
        _away_kernel,
        half,
        [*fishers, *mats],
        [_rows(height, width)] * 4 + [mat_spec] * 4,
        [jax.ShapeDtypeStruct((2, height, width), BF16)],
        [_pair(height, width)],
    )[0]


def merged(half, near, both_far, down_far, both_line, down_line, gate_back, up_back, down_back):
    steps = 2
    return _call(
        _merge_kernel,
        half,
        [*near, both_far, *near, down_far, *both_line, *down_line, gate_back, up_back, down_back],
        [_rows(512, 512, 0, steps)] * 4
        + [_rows(256, 512, 512 // (256 // steps), steps)] * 3
        + [_rows(256, 512, 0, steps)]
        + [_half_rows(512, 512, 0, steps)] * 4
        + [_half_columns(256, 512, steps)] * 4
        + [_pair(512, 256, steps), _pair(512, 256, steps), _pair(256, 512, steps)],
        [
            jax.ShapeDtypeStruct((512, 256), F32),
            jax.ShapeDtypeStruct((512, 256), F32),
            jax.ShapeDtypeStruct((256, 512), F32),
        ],
        [_rows(512, 256, 0, steps), _rows(512, 256, 0, steps), _rows(256, 512, 0, steps)],
        steps,
    )


def body(inputs, targets, gain, w_gate, w_up, w_down):
    gain_row = gain[0]
    down_mat = w_down[0]
    width = inputs.shape[3]
    scale_model = 1.0 / math.sqrt(width)
    scale_hidden = 1.0 / math.sqrt(w_down.shape[1] * 32)
    core = lax.axis_index("fsdp") % 2
    branch = lax.axis_index("branch")
    y_at, zh_at = branch // 2, branch % 2
    zh_own = jnp.reshape(zh_at, (1,)).astype(jnp.int32)
    zh_away = 1 - zh_own

    def slot_of(by):
        return (y_at + by) % 4

    def slices(mat, axis):
        return [
            lax.dynamic_slice_in_dim(mat, slot_of(by) * 1024, 1024, axis) for by in (0,) + RELATIVE
        ]

    def fetch(part, by):
        return shift(part, "y", by)

    x_pair = pair_up(inputs[0], core)
    down_parts = slices(down_mat, 1)
    down_near = [fetch(part, by) for by, part in zip(RELATIVE, down_parts[1:3])]
    line = gather_line(x_pair)
    line, target_rows, down_far = tie(line, targets[0], down_parts[3])
    target_pair = pair_up(target_rows, core)
    down_far = fetch(down_far, 2)
    last_line, down_near = tie(line, down_near)
    tokens = jnp.stack(
        [line] + [shift(last_line if by == 1 else line, "x", by) for by in RELATIVE]
    )
    both_mat = jnp.concatenate([w_gate[0], w_up[0]], axis=1)
    tokens, target_pair, down_far, both_mat = tie(tokens, target_pair, down_far, both_mat)
    down_line = [down_parts[0]] + down_near + [down_far]
    both_parts = slices(both_mat, 0)
    near = [fetch(part, by) for by, part in zip(RELATIVE, both_parts[1:3])]
    tokens = [tokens, shift(tokens, "core", 1)]

    def times(left, mat, scale):
        return jnp.einsum("xkmd,df->xkmf", left, mat, preferred_element_type=F32) * scale

    def forward(rows):
        pre = times(rows, both_mat, scale_model)
        gate_pre, up_pre = pre[..., :256], pre[..., 256:]
        hidden = (gate_pre * jax.nn.sigmoid(gate_pre) * up_pre).astype(BF16)
        return pre, hidden, times(hidden, down_mat, scale_hidden).astype(BF16)

    steps = [forward(rows) for rows in tokens]
    hiddens = [step[1] for step in steps]
    chip = (steps[0][2].astype(F32) + shift(steps[1][2], "core", 1).astype(F32)).astype(BF16)
    chip = scatter([chip[i] for i in range(4)], "x")
    chip, far = tie(chip, both_parts[3])
    far = fetch(far, 2)
    parts = [chip[:, 8 * i : 8 * i + 8] for i in range(4)]
    parts[1], near = tie(parts[1], near)
    summed = scatter(parts, "zl")
    out_rows = x_pair.astype(F32) + summed.astype(F32)
    grad_local = norm_grad(out_rows, target_pair.astype(F32), gain_row)
    grads = jnp.zeros((4,) + line.shape, BF16)
    for i, piece in enumerate(gather(gather_line(grad_local), "x")):
        grads = lax.dynamic_update_index_in_dim(grads, piece, i, 0)
    grads, far = tie(grads, far)
    both_line = [both_parts[0]] + near + [far]

    def backward(grad_out, pre):
        grad_hidden = (
            jnp.einsum("xkmd,fd->xkmf", grad_out, down_mat, preferred_element_type=F32)
            * scale_hidden
        )
        gate_pre, up_pre = pre[..., :256], pre[..., 256:]
        sig = jax.nn.sigmoid(gate_pre)
        d_gate = grad_hidden * up_pre * sig * (1.0 + gate_pre * (1.0 - sig))
        return d_gate.astype(BF16), (grad_hidden * gate_pre * sig).astype(BF16)

    other = shift(grads, "core", 1)
    other, d_own = tie(other, backward(grads, steps[0][0]))
    grads = [grads, other]

    def blocks(half, *jobs, places=RELATIVE + (0,)):
        slots = jnp.concatenate([2 * slot_of(by) + half for by in places])
        return fisher_blocks(slots, *jobs)

    def exchange(parts):
        return [parts[3]] + [shift(part, "y", by) for by, part in zip(RELATIVE, parts)]

    down_away = blocks(zh_away, (hiddens, grads, scale_hidden, 1), places=RELATIVE)
    grads, down_away = tie(grads, down_away)
    kept = blocks(zh_away, (hiddens, grads, scale_hidden, 1), places=(0,))
    down_away = exchange([*down_away, *kept])

    d_other = backward(grads[1], steps[1][0])
    d_gates, d_ups = [d_own[0], d_other[0]], [d_own[1], d_other[1]]
    gate_away = blocks(zh_away, (tokens, d_gates, scale_model, 0))

    near_away, gate_away, hiddens, grads, tokens, d_gates, d_ups = tie(
        down_away[1:3], gate_away, hiddens, grads, tokens, d_gates, d_ups
    )
    gate_away = exchange(gate_away)
    down_sent = leaving(
        zh_away, [down_away[0], *near_away, down_away[3]], down_line, _half_columns(256, 512)
    )
    down_sent, tokens, d_ups = tie(down_sent, tokens, d_ups)
    down_back = shift(down_sent, "zh", 1)
    up_away = blocks(zh_away, (tokens, d_ups, scale_model, 0))

    near_away, up_away, hiddens, grads, tokens, d_gates, d_ups = tie(
        gate_away[1:3], up_away, hiddens, grads, tokens, d_gates, d_ups
    )
    up_away = exchange(up_away)
    gate_sent = leaving(
        zh_away, [gate_away[0], *near_away, gate_away[3]], both_line, _half_rows(512, 256)
    )
    gate_sent, hiddens, grads, tokens, d_gates, d_ups = tie(
        gate_sent, hiddens, grads, tokens, d_gates, d_ups
    )
    gate_back = shift(gate_sent, "zh", 1)
    d_both = [jnp.concatenate(pair, axis=-1) for pair in zip(d_gates, d_ups)]
    own = blocks(
        zh_own, (tokens, d_both, scale_model, 0), (hiddens, grads, scale_hidden, 1)
    )

    up_away, own, down_back = tie(up_away, own, down_back)
    up_sent = leaving(zh_away, up_away, both_line, _half_rows(512, 256, 1))
    up_sent, own = tie(up_sent, own)
    last_own, gate_back = tie(own[2][512:], gate_back)
    both_far, down_far = shift(own[2][:512], "y", 2), shift(last_own, "y", 2)
    up_back = shift(up_sent, "zh", 1)
    near_own = [own[3]] + [shift(part, "y", by) for by, part in zip(RELATIVE, own[:2])]
    gate, up, down = merged(zh_own, near_own, both_far, down_far, both_line, down_line, gate_back, up_back, down_back)
    return gate, up, down


def solution(mesh):
    placed = (
        P("branch", None, "fsdp", None),
        P("branch", None, "fsdp", None),
        P("branch", None),
        P("branch", None, "fsdp"),
        P("branch", None, "fsdp"),
        P("branch", "fsdp", None),
    )
    return jax.shard_map(
        body,
        mesh=mesh,
        in_specs=placed,
        out_specs=(P("branch", "fsdp"), P("branch", "fsdp"), P("fsdp", "branch")),
        check_vma=False,
    )
```
